32 devices in a mesh: wide: 4 (over y, x), narrow: 8 (over z, core).
Axes of the slice: x: 2, y: 2, z: 4, core: 2. Of those that a mesh axis runs over, the one named last changes fastest.
Arguments:
- volume_field: float32 [2, 8, 64, 128, 512], P(None, None, 'wide', 'narrow'), may hold values from -6 to 6
- coefficients: bfloat16 [3, 64, 128, 512], P(None, 'wide', 'narrow'), may hold values from 0.25 to 1
- density: float32 [2, 8, 65536], P(None, None, 'narrow'), may hold values from -6 to 6
- boundary_matrix: bfloat16 [2, 4, 256, 65536], P(None, None, 'wide', 'narrow'), may hold values from -0.03125 to 0.03125
- upsample: int32 [128], P('narrow'), may hold values from 1 to 4, as said below
- trace_cell: int32 [4, 8, 256], P('wide', 'narrow'), may hold values from 0 to 255
- trace_row: int32 [4, 8, 256], P('wide', 'narrow'), may hold values from 0 to 255, as said below
- slot_counts: int32 [4, 8], P('wide', 'narrow'), may hold values from 192 to 256, as said below
Outputs:
- volume_out: float32 [2, 8, 64, 128, 512], P(None, None, 'wide', 'narrow')
- boundary_out: float32 [2, 8, 256], P(None, None, ('wide', 'narrow'))
The draws below stay inside these ranges and needn't reach their ends.
Inputs may be any that keep to these rules, and one draw needn't show every extreme that they name: `trace_row`: live slots of one brick name rows of one owner (rows k * 8 to (k + 1) * 8 - 1) at most 16 times; in every draw one owner is named 16 times by the live slots of every brick. `slot_counts`: some brick has all 256 slots live. `upsample`: some panel group has factor 4 and some has factor 1.
All inputs are finite; a program needn't handle non-finite values.
Results may differ from the reference program's by a relative error of at most 0.0019.
Values sent between devices are 32-bit elements; how exact they have to be, the bound alone decides.
A program may use at most 192 MiB of HBM per device.

```python
import jax
import jax.numpy as jnp
from jax import lax

W = 8
CX = 16
CY = 16
NZ = 512
NB = 65536
COLS_BLK = 512
UMAX = 4
TSLOTS = 256
CAP = 16
NX = 64
NY = 128
ROWS = 256
RPD = 8
BLOCKS = 128
N_WIDE = 4
N_NARROW = 8


def slot_plan(key):
    device_count = N_WIDE * N_NARROW
    key_hot, key_bricks, key_full = jax.random.split(key, 3)
    hottest = jax.random.randint(key_hot, (), 0, device_count)
    full_brick = jax.random.randint(key_full, (), 0, device_count)

    def one_brick(brick_key, brick):
        key_order, key_count, key_shuffle, key_local = jax.random.split(brick_key, 4)
        order = jax.random.permutation(key_order, CAP * (device_count - 1))[:TSLOTS - CAP]
        owner_rest = (hottest + 1 + order % (device_count - 1)) % device_count
        owners = jnp.concatenate([jnp.full((CAP,), hottest, jnp.int32), owner_rest.astype(jnp.int32)])
        live_count = jax.random.randint(key_count, (), 3 * TSLOTS // 4, TSLOTS + 1)
        live_count = jnp.where(brick == full_brick, TSLOTS, live_count)
        position = jnp.arange(TSLOTS, dtype=jnp.int32)
        scores = jax.random.randint(key_shuffle, (TSLOTS,), 0, TSLOTS) * TSLOTS + position
        scores = jnp.where(position < live_count, scores, TSLOTS * TSLOTS + position)
        shuffled = jnp.argsort(scores, stable=True)
        owners = owners[shuffled]
        local_row = jax.random.randint(key_local, (TSLOTS,), 0, RPD)
        return ((owners * RPD + local_row).astype(jnp.int32), live_count.astype(jnp.int32))
    brick_keys = jax.random.split(key_bricks, device_count)
    slot_rows, live_counts = jax.vmap(one_brick)(brick_keys, jnp.arange(device_count, dtype=jnp.int32))
    return (slot_rows.reshape(N_WIDE, N_NARROW, TSLOTS), live_counts.reshape(N_WIDE, N_NARROW))


def draw_trace_row(key, part):
    return slot_plan(jax.random.fold_in(key, 7))[0]


def draw_slot_counts(key, part):
    return slot_plan(jax.random.fold_in(key, 7))[1]


def draw_upsample(key, part):
    key_base, key_start = jax.random.split(key)
    base = jax.random.randint(key_base, (BLOCKS,), 1, 3)
    start = jax.random.randint(key_start, (), 0, BLOCKS)
    run_length = max(BLOCKS // 8, 1)
    position = (jnp.arange(BLOCKS, dtype=jnp.int32) - start) % BLOCKS
    values = jnp.where(position < run_length, UMAX, base)
    values = jnp.where(position == run_length, 1, values)
    return values.astype(jnp.int32)


def plant(drawn, stream_key, low, largest):
    shape = drawn.shape
    index_at = [jax.random.randint(jax.random.fold_in(stream_key, axis), (), 0, shape[axis]) for axis in range(len(shape))]
    drawn = drawn.at[tuple(index_at)].set(low)
    longest = shape.index(max(shape))
    index_at[longest] = (index_at[longest] + 1) % shape[longest]
    return drawn.at[tuple(index_at)].set(largest)


def strengthened(entries, own_key, source, target, blocks, factor):
    owner, partner = [(jnp.arange(entries.shape[axis_at]) // (entries.shape[axis_at] // blocks)).reshape([-1 if axis == axis_at else 1 for axis in range(entries.ndim)]) for axis_at in (source, target)]
    chosen = jax.random.permutation(own_key, blocks)[partner]
    strong = (owner == chosen) | (owner == (partner + blocks // 2) % blocks)
    return jnp.where(strong, factor * entries, entries)


def levels(rng, extent, pieces, low, largest):
    def one(axis_at, parts):
        steps = jax.random.uniform(jax.random.fold_in(jax.random.fold_in(rng, 6), axis_at), (parts,), jnp.float32, low / len(pieces), largest / len(pieces))
        return jnp.repeat(jnp.exp(steps), extent[axis_at] // parts).reshape((-1,) + (1,) * (len(extent) - axis_at - 1))

    factor_of = one(*pieces[0])
    for cut in pieces[1:]:
        factor_of = factor_of * one(*cut)
    return factor_of


def centred(stream_key, extent, scale, most, pieces=(), held_as=jnp.bfloat16):
    values = jax.random.normal(stream_key, extent, jnp.float32) * scale
    if len(pieces) > 0:
        values = levels(stream_key, extent, pieces, -0.22, 0.18) * values
    return jnp.clip(values, min=-most, max=most).astype(held_as)


def heavy_noise(rng, shape, spread, most, cuts, heavy, kind=jnp.bfloat16):
    drawn = spread * jax.random.normal(rng, shape, jnp.float32)
    if cuts:
        drawn = drawn * levels(rng, shape, cuts, -0.22, 0.18)
    return jnp.clip(strengthened(drawn, jax.random.fold_in(rng, 3), *heavy), -most, most).astype(kind)


def setup_inputs(seed: int = 0) -> dict:
    arg_keys = jax.random.split(jax.random.key(seed), 9)
    volume_field = centred(arg_keys[0], (2, W, NX, NY, NZ), 1.0, 6.0, ((2, 4), (3, 8)), jnp.float32)
    coefficients = jnp.clip(0.25 + 0.75 * jax.random.uniform(arg_keys[1], (3, NX, NY, NZ), jnp.float32) ** levels(arg_keys[1], (3, NX, NY, NZ), ((1, 4), (2, 8)), -0.2, 0.2), 0.25, 1.0).astype(jnp.bfloat16)
    density = centred(arg_keys[2], (2, W, NB), 1.0, 6.0, ((2, 8),), jnp.float32)
    boundary_matrix = heavy_noise(arg_keys[3], (2, UMAX, ROWS, NB), NB ** -0.5, 0.03125, ((2, 4), (3, 8)), (3, 2, 8, 2.0))
    upsample = draw_upsample(jax.random.fold_in(arg_keys[8], 71), 0)
    trace_cell = plant(jax.random.randint(arg_keys[5], (N_WIDE, N_NARROW, TSLOTS), 0, CX * CY), jax.random.fold_in(arg_keys[5], 1), 0, (CX * CY) - 1).astype(jnp.int32)
    trace_row = draw_trace_row(jax.random.fold_in(arg_keys[8], 71), 0)
    slot_counts = draw_slot_counts(jax.random.fold_in(arg_keys[8], 71), 0)
    return {"volume_field": volume_field, "coefficients": coefficients, "density": density, "boundary_matrix": boundary_matrix, "upsample": upsample, "trace_cell": trace_cell, "trace_row": trace_row, "slot_counts": slot_counts}


def channel_stiffness(plane):
    padded = jnp.pad(plane, 1)
    size_x, size_y, size_z = plane.shape
    edge_sum = jnp.zeros(plane.shape, jnp.float32)
    corner_sum = jnp.zeros(plane.shape, jnp.float32)
    for across in (-1, 0, 1):
        for along in (-1, 0, 1):
            for upward in (-1, 0, 1):
                moved = abs(across) + abs(along) + abs(upward)
                if moved < 2:
                    continue
                shifted = padded[1 + across:1 + across + size_x, 1 + along:1 + along + size_y, 1 + upward:1 + upward + size_z]
                if moved == 2:
                    edge_sum = edge_sum + shifted
                else:
                    corner_sum = corner_sum + shifted
    return (8.0 / 3.0) * plane - edge_sum / 6.0 - corner_sum / 12.0


def reference(volume_field, coefficients, density, boundary_matrix, upsample, trace_cell, trace_row, slot_counts):
    channels = volume_field.reshape(2 * W, NX, NY, NZ)
    stiffness = lax.map(channel_stiffness, channels).reshape(volume_field.shape)
    scales = coefficients.astype(jnp.float32)
    turned = jnp.stack([volume_field[1], -volume_field[0]])
    operated = scales[0] * stiffness - scales[1] * volume_field + scales[2] * turned

    blocks_density = density.reshape(2 * W, BLOCKS, COLS_BLK)
    following = jnp.concatenate([blocks_density[:, :, 1:], blocks_density[:, :, -1:]], axis=2)
    factor = upsample.astype(jnp.float32)[None, :, None]
    products = jnp.zeros((2 * ROWS, 2 * W), jnp.float32)
    for level_index in range(UMAX):
        blend = level_index / factor
        fine = jnp.where(level_index < upsample[None, :, None], ((1.0 - blend) * blocks_density + blend * following) / factor, 0.0)
        fine = fine.reshape(2 * W, NB).astype(jnp.bfloat16)
        matrix = boundary_matrix[:, level_index].reshape(2 * ROWS, NB)
        products = products + lax.dot_general(matrix, fine, (((1,), (1,)), ((), ())), preferred_element_type=jnp.float32)
    real_rows = products[:ROWS, :W] - products[ROWS:, W:]
    imag_rows = products[:ROWS, W:] + products[ROWS:, :W]
    bem_rows = jnp.concatenate([real_rows, imag_rows], axis=1)

    slot_index = jnp.arange(TSLOTS, dtype=jnp.int32)
    live_mask = (slot_index[None, None, :] < slot_counts[:, :, None]).reshape(-1)
    cell_x = (jnp.arange(N_WIDE, dtype=jnp.int32)[:, None, None] * CX + trace_cell // CY).reshape(-1)
    cell_y = (jnp.arange(N_NARROW, dtype=jnp.int32)[None, :, None] * CY + trace_cell % CY).reshape(-1)
    slot_rows = trace_row.reshape(-1).astype(jnp.int32)
    top_plane = volume_field[:, :, :, :, NZ - 1].reshape(2 * W, NX * NY)
    cell_ids = (cell_x * NY + cell_y).astype(jnp.int32)
    slot_values = jnp.where(live_mask[:, None], top_plane[:, cell_ids].T, 0.0)
    trace_sum = jax.ops.segment_sum(slot_values, slot_rows, num_segments=ROWS)
    boundary_out = (bem_rows - 0.25 * trace_sum).T.reshape(2, W, ROWS)

    sent_back = jnp.where(live_mask[:, None], bem_rows[slot_rows], 0.0)
    cell_add = jax.ops.segment_sum(sent_back, cell_ids, num_segments=NX * NY)
    cell_add = cell_add.T.reshape(2, W, NX, NY)
    volume_out = operated.at[:, :, :, :, NZ - 1].add(cell_add)
    return volume_out, boundary_out
```

```python
import functools

import jax
import jax.numpy as jnp
from jax import lax
from jax.experimental import pallas as pl
from jax.experimental.pallas import tpu as pltpu
from jax.sharding import PartitionSpec as P

UMAX = 4
BOTH = ("wide", "narrow")


def shifts(axis):
    peers = lax.axis_size(axis)
    up = [(i, i + 1) for i in range(peers - 1)]
    return up, [(j, i) for i, j in up]


def bem_kernel(keep_ref, next_ref, density_ref, matrix_ref, out_ref, *, groups, width):
    step = pl.program_id(0)
    waves = density_ref.shape[1]
    rows = matrix_ref.shape[2]
    lane = lax.broadcasted_iota(jnp.int32, (2 * waves, width), 1)
    total = jnp.zeros((2 * waves, 2 * rows), jnp.float32)
    for g in range(groups):
        columns = pl.ds(g * width, width)
        own = density_ref[:, :, columns].reshape(2 * waves, width)
        after = jnp.where(lane == width - 1, own, pltpu.roll(own, width - 1, axis=1))
        for level in range(UMAX):
            at = step * groups + g
            fine = keep_ref[level, at] * own + next_ref[level, at] * after
            matrix = matrix_ref[:, level, :, columns].reshape(2 * rows, width)
            total = total + lax.dot_general(
                fine.astype(jnp.bfloat16),
                matrix,
                (((1,), (1,)), ((), ())),
                preferred_element_type=jnp.float32,
            )
    real = total[:waves, :rows] - total[waves:, rows:]
    imag = total[waves:, :rows] + total[:waves, rows:]
    packed = jnp.concatenate([real, imag], axis=1)

    @pl.when(step == 0)
    def _():
        out_ref[...] = packed

    @pl.when(step > 0)
    def _():
        out_ref[...] += packed


def bem_partial(density, boundary_matrix, upsample):
    parts, waves, columns = density.shape
    rows = boundary_matrix.shape[2]
    blocks = upsample.shape[0]
    width = columns // blocks
    groups = 4 if blocks % 4 == 0 else 1
    factor = upsample.astype(jnp.float32)[None, :]
    level = jnp.arange(UMAX, dtype=jnp.int32)[:, None]
    blend = level.astype(jnp.float32) / factor
    used = level < upsample[None, :]
    keep = jnp.where(used, (1.0 - blend) / factor, 0.0)
    following = jnp.where(used, blend / factor, 0.0)


    return pl.pallas_call(
        functools.partial(bem_kernel, groups=groups, width=width),
        grid=(blocks // groups,),
        in_specs=[
            pl.BlockSpec(memory_space=pltpu.SMEM),
            pl.BlockSpec(memory_space=pltpu.SMEM),
            pl.BlockSpec((parts, waves, groups * width), lambda i: (0, 0, i)),
            pl.BlockSpec((2, UMAX, rows, groups * width), lambda i: (0, 0, 0, i)),
        ],
        out_specs=pl.BlockSpec((waves, 2 * rows), lambda i: (0, 0)),
        out_shape=jax.ShapeDtypeStruct((waves, 2 * rows), jnp.float32),
        compiler_params=pltpu.CompilerParams(
            vmem_limit_bytes=40 * 1024 * 1024, dimension_semantics=("arbitrary",)
        ),
        cost_estimate=pl.CostEstimate(
            flops=2 * UMAX * 4 * waves * rows * columns,
            bytes_accessed=boundary_matrix.size * 2 + density.size * 4,
            transcendentals=0,
        ),
        name="boundary_product",
    )(keep, following, density, boundary_matrix)


def stencil_kernel(
    volume_ref, x_lo, x_hi, y_lo, y_hi, scale_ref, add_ref, out_ref, across_ref
):
    wave = pl.program_id(0)
    waves = pl.num_programs(0)
    size_x, size_y, size_z = volume_ref.shape[2:]
    shape = (size_y, size_z)
    row = lax.broadcasted_iota(jnp.int32, shape, 0)
    lane = lax.broadcasted_iota(jnp.int32, shape, 1)
    channel_lane = lax.broadcasted_iota(jnp.int32, (size_y, add_ref.shape[1]), 1)

    def sum_y(plane, part, at):
        before = y_lo[part, 0, pl.ds(at, 1), :]
        after = y_hi[part, 0, pl.ds(at, 1), :]
        up = jnp.where(row == 0, before, pltpu.roll(plane, 1, axis=0))
        down = jnp.where(row == size_y - 1, after, pltpu.roll(plane, size_y - 1, axis=0))
        return up + down

    for part in range(2):
        across_ref[part, 0] = sum_y(x_lo[part, 0], part, 0)
        across_ref[part, size_x + 1] = sum_y(x_hi[part, 0], part, size_x + 1)

    def first(x, carry):
        for part in range(2):
            across_ref[part, x + 1] = sum_y(volume_ref[part, 0, x], part, x + 1)
        return carry

    lax.fori_loop(0, size_x, first, 0)

    def emit(x, before, after):
        scale0 = scale_ref[0, x].astype(jnp.float32)
        scale1 = scale_ref[1, x].astype(jnp.float32)
        scale2 = scale_ref[2, x].astype(jnp.float32)
        own = [volume_ref[part, 0, x] for part in range(2)]
        for part in range(2):
            outer = across_ref[part, x] + across_ref[part, x + 2]
            inner = outer + 2.0 * (before[part] + after[part] + across_ref[part, x + 1])
            left = jnp.where(lane == 0, 0.0, pltpu.roll(inner, 1, axis=1))
            right = jnp.where(lane == size_z - 1, 0.0, pltpu.roll(inner, size_z - 1, axis=1))
            total = left + right + 2.0 * outer
            stiffness = (8.0 / 3.0) * own[part] - total * (1.0 / 12.0)
            turned = own[1] if part == 0 else -own[0]
            value = scale0 * stiffness - scale1 * own[part] + scale2 * turned
            tile = add_ref[pl.ds(x * size_y, size_y), :]
            added = jnp.sum(
                jnp.where(channel_lane == part * waves + wave, tile, 0.0), axis=1, keepdims=True
            )
            out_ref[part, 0, x] = value + jnp.where(lane == size_z - 1, added, 0.0)

    both = range(2)
    emit(0, [x_lo[p, 0] for p in both], [volume_ref[p, 0, 1] for p in both])

    def second(x, carry):
        emit(
            x,
            [volume_ref[p, 0, x - 1] for p in both],
            [volume_ref[p, 0, x + 1] for p in both],
        )
        return carry

    lax.fori_loop(1, size_x - 1, second, 0)
    emit(
        size_x - 1,
        [volume_ref[p, 0, size_x - 2] for p in both],
        [x_hi[p, 0] for p in both],
    )


def stencil(volume, x_lo, x_hi, y_lo, y_hi, coefficients, cell_add):
    parts, waves, size_x, size_y, size_z = volume.shape
    whole = pl.BlockSpec((parts, 1, size_x, size_y, size_z), lambda w: (0, w, 0, 0, 0))
    face_x = pl.BlockSpec((parts, 1, size_y, size_z), lambda w: (0, w, 0, 0))
    face_y = pl.BlockSpec((parts, 1, size_x + 2, size_z), lambda w: (0, w, 0, 0))
    return pl.pallas_call(
        stencil_kernel,
        grid=(waves,),
        in_specs=[
            whole,
            face_x,
            face_x,
            face_y,
            face_y,
            pl.BlockSpec(coefficients.shape, lambda w: (0, 0, 0, 0)),
            pl.BlockSpec(cell_add.shape, lambda w: (0, 0)),
        ],
        out_specs=whole,
        out_shape=jax.ShapeDtypeStruct(volume.shape, jnp.float32),
        scratch_shapes=[pltpu.VMEM((parts, size_x + 2, size_y, size_z), jnp.float32)],
        compiler_params=pltpu.CompilerParams(
            vmem_limit_bytes=40 * 1024 * 1024, dimension_semantics=("arbitrary",)
        ),
        cost_estimate=pl.CostEstimate(
            flops=volume.size * 40, bytes_accessed=volume.size * 8, transcendentals=0
        ),
        name="volume_rows",
    )(volume, x_lo, x_hi, y_lo, y_hi, coefficients, cell_add)


def on_device(
    volume_field,
    coefficients,
    density,
    boundary_matrix,
    upsample,
    trace_cell,
    trace_row,
    slot_counts,
):
    parts, waves, size_x, size_y, size_z = volume_field.shape
    n_wide, n_narrow = lax.axis_size("wide"), lax.axis_size("narrow")
    group_rows = boundary_matrix.shape[2]
    all_rows = n_wide * group_rows
    rows_each = group_rows // n_narrow

    up, down = shifts("wide")
    x_lo = lax.ppermute(volume_field[:, :, -1], "wide", up)
    x_hi = lax.ppermute(volume_field[:, :, 0], "wide", down)

    def y_face(at):
        return jnp.concatenate(
            [x_lo[:, :, at][:, :, None], volume_field[:, :, :, at], x_hi[:, :, at][:, :, None]],
            axis=2,
        )

    up, down = shifts("narrow")
    y_lo = lax.ppermute(y_face(size_y - 1), "narrow", up)
    y_hi = lax.ppermute(y_face(0), "narrow", down)

    slots = trace_row.shape[2]
    live = jnp.arange(slots, dtype=jnp.int32) < slot_counts.reshape(())
    slot_rows = jnp.where(live, trace_row.reshape(slots), -1)
    slot_cells = trace_cell.reshape(slots)
    row_hot = (slot_rows[None, :] == jnp.arange(all_rows, dtype=jnp.int32)[:, None]).astype(
        jnp.bfloat16
    )
    cell_hot = (
        slot_cells[None, :] == jnp.arange(size_x * size_y, dtype=jnp.int32)[:, None]
    ).astype(jnp.bfloat16)
    counts = lax.dot_general(
        cell_hot, row_hot, (((1,), (1,)), ((), ())), preferred_element_type=jnp.float32
    )
    top = volume_field[:, :, :, :, -1].reshape(parts * waves, size_x * size_y)
    trace_part = jnp.dot(top, counts, precision=lax.Precision.HIGHEST)
    trace_part = trace_part.reshape(parts * waves, n_wide * n_narrow, rows_each)
    trace_part = trace_part.transpose(1, 0, 2).reshape(n_wide * n_narrow, -1)
    trace_sum = lax.psum_scatter(trace_part, BOTH, scatter_dimension=0, tiled=True)
    trace_sum = trace_sum.reshape(parts * waves, rows_each)

    partial_rows = bem_partial(density, boundary_matrix, upsample)
    gathered = lax.all_gather(partial_rows, BOTH, axis=0, tiled=False)
    summed = jnp.sum(gathered.reshape(n_wide, n_narrow, waves, 2, group_rows), axis=1)
    bem_rows = summed.transpose(2, 1, 0, 3).reshape(parts * waves, all_rows)
    start = (lax.axis_index("wide") * n_narrow + lax.axis_index("narrow")) * rows_each
    own_rows = lax.dynamic_slice_in_dim(bem_rows, start, rows_each, 1)
    boundary_out = (own_rows - 0.25 * trace_sum).reshape(parts, waves, rows_each)
    cell_add = lax.dot_general(
        counts, bem_rows, (((1,), (1,)), ((), ())), precision=lax.Precision.HIGHEST
    )
    volume_out = stencil(volume_field, x_lo, x_hi, y_lo, y_hi, coefficients, cell_add)
    return (volume_out, boundary_out)


def solution(mesh):
    return jax.shard_map(
        on_device,
        mesh=mesh,
        in_specs=(
            P(None, None, "wide", "narrow", None),
            P(None, "wide", "narrow", None),
            P(None, None, "narrow"),
            P(None, None, "wide", "narrow"),
            P("narrow"),
            P("wide", "narrow", None),
            P("wide", "narrow", None),
            P("wide", "narrow"),
        ),
        out_specs=(P(None, None, "wide", "narrow", None), P(None, None, ("wide", "narrow"))),
        check_vma=False,
    )
```

```python
import functools

import jax
import jax.numpy as jnp
from jax import lax
from jax.experimental import pallas as pl
from jax.experimental.pallas import tpu as pltpu
from jax.sharding import PartitionSpec as P

UMAX = 4
BOTH = ("wide", "narrow")


def shifts(axis):
    peers = lax.axis_size(axis)
    up = [(i, i + 1) for i in range(peers - 1)]
    return up, [(j, i) for i, j in up]


def bem_kernel(keep_ref, next_ref, density_ref, matrix_ref, out_ref, *, groups, width):
    step = pl.program_id(0)
    waves = density_ref.shape[1]
    rows = matrix_ref.shape[2]
    lane = lax.broadcasted_iota(jnp.int32, (2 * waves, width), 1)
    total = jnp.zeros((2 * waves, 2 * rows), jnp.float32)
    for g in range(groups):
        columns = pl.ds(g * width, width)
        own = density_ref[:, :, columns].reshape(2 * waves, width)
        after = jnp.where(lane == width - 1, own, pltpu.roll(own, width - 1, axis=1))
        for level in range(UMAX):
            at = step * groups + g
            fine = keep_ref[level, at] * own + next_ref[level, at] * after
            matrix = matrix_ref[:, level, :, columns].reshape(2 * rows, width)
            total = total + lax.dot_general(
                fine.astype(jnp.bfloat16),
                matrix,
                (((1,), (1,)), ((), ())),
                preferred_element_type=jnp.float32,
            )
    real = total[:waves, :rows] - total[waves:, rows:]
    imag = total[waves:, :rows] + total[:waves, rows:]
    packed = jnp.concatenate([real, imag], axis=1)

    @pl.when(step == 0)
    def _():
        out_ref[...] = packed

    @pl.when(step > 0)
    def _():
        out_ref[...] += packed


def bem_partial(density, boundary_matrix, upsample):
    parts, waves, columns = density.shape
    rows = boundary_matrix.shape[2]
    blocks = upsample.shape[0]
    width = columns // blocks
    groups = 4 if blocks % 4 == 0 else 1
    factor = upsample.astype(jnp.float32)[None, :]
    level = jnp.arange(UMAX, dtype=jnp.int32)[:, None]
    blend = level.astype(jnp.float32) / factor
    used = level < upsample[None, :]
    keep = jnp.where(used, (1.0 - blend) / factor, 0.0)
    following = jnp.where(used, blend / factor, 0.0)


    return pl.pallas_call(
        functools.partial(bem_kernel, groups=groups, width=width),
        grid=(blocks // groups,),
        in_specs=[
            pl.BlockSpec(memory_space=pltpu.SMEM),
            pl.BlockSpec(memory_space=pltpu.SMEM),
            pl.BlockSpec((parts, waves, groups * width), lambda i: (0, 0, i)),
            pl.BlockSpec((2, UMAX, rows, groups * width), lambda i: (0, 0, 0, i)),
        ],
        out_specs=pl.BlockSpec((waves, 2 * rows), lambda i: (0, 0)),
        out_shape=jax.ShapeDtypeStruct((waves, 2 * rows), jnp.float32),
        compiler_params=pltpu.CompilerParams(
            vmem_limit_bytes=40 * 1024 * 1024, dimension_semantics=("arbitrary",)
        ),
        cost_estimate=pl.CostEstimate(
            flops=2 * UMAX * 4 * waves * rows * columns,
            bytes_accessed=boundary_matrix.size * 2 + density.size * 4,
            transcendentals=0,
        ),
        name="boundary_product",
    )(keep, following, density, boundary_matrix)


def stencil_kernel(
    volume_ref, x_lo, x_hi, y_lo, y_hi, edge_lo, edge_hi, scale_ref, out_ref, across_ref
):
    size_x, size_y, size_z = volume_ref.shape[2:]
    shape = (size_y, size_z)
    row = lax.broadcasted_iota(jnp.int32, shape, 0)
    lane = lax.broadcasted_iota(jnp.int32, shape, 1)

    def sum_y(plane, before, after):
        up = jnp.where(row == 0, before, pltpu.roll(plane, 1, axis=0))
        down = jnp.where(row == size_y - 1, after, pltpu.roll(plane, size_y - 1, axis=0))
        return up + down

    for part in range(2):
        for side, face, at in ((0, x_lo, 0), (1, x_hi, size_x + 1)):
            across_ref[part, at] = sum_y(
                face[part, 0], edge_lo[part, 0, side : side + 1], edge_hi[part, 0, side : side + 1]
            )

    def first(x, carry):
        for part in range(2):
            across_ref[part, x + 1] = sum_y(
                volume_ref[part, 0, x],
                y_lo[part, 0, pl.ds(x, 1), :],
                y_hi[part, 0, pl.ds(x, 1), :],
            )
        return carry

    lax.fori_loop(0, size_x, first, 0)

    def emit(x, before, after):
        scale0 = scale_ref[0, x].astype(jnp.float32)
        scale1 = scale_ref[1, x].astype(jnp.float32)
        scale2 = scale_ref[2, x].astype(jnp.float32)
        own = [volume_ref[part, 0, x] for part in range(2)]
        for part in range(2):
            outer = across_ref[part, x] + across_ref[part, x + 2]
            inner = outer + 2.0 * (before[part] + after[part] + across_ref[part, x + 1])
            left = jnp.where(lane == 0, 0.0, pltpu.roll(inner, 1, axis=1))
            right = jnp.where(lane == size_z - 1, 0.0, pltpu.roll(inner, size_z - 1, axis=1))
            total = left + right + 2.0 * outer
            stiffness = (8.0 / 3.0) * own[part] - total * (1.0 / 12.0)
            turned = own[1] if part == 0 else -own[0]
            out_ref[part, 0, x] = scale0 * stiffness - scale1 * own[part] + scale2 * turned

    both = range(2)
    emit(0, [x_lo[p, 0] for p in both], [volume_ref[p, 0, 1] for p in both])

    def second(x, carry):
        emit(
            x,
            [volume_ref[p, 0, x - 1] for p in both],
            [volume_ref[p, 0, x + 1] for p in both],
        )
        return carry

    lax.fori_loop(1, size_x - 1, second, 0)
    emit(
        size_x - 1,
        [volume_ref[p, 0, size_x - 2] for p in both],
        [x_hi[p, 0] for p in both],
    )


def top_kernel(operated_ref, add_ref, out_ref):
    wave = pl.program_id(0)
    waves = pl.num_programs(0)
    size_x, size_y, size_z = operated_ref.shape[2:]
    cells = size_x * size_y
    channel = lax.broadcasted_iota(jnp.int32, (cells, add_ref.shape[1]), 1)
    lane = lax.broadcasted_iota(jnp.int32, (cells, size_z), 1)
    for part in range(2):
        added = jnp.sum(
            jnp.where(channel == part * waves + wave, add_ref[...], 0.0), axis=1, keepdims=True
        )
        own = operated_ref[part, 0].reshape(cells, size_z)
        total = own + jnp.where(lane == size_z - 1, added, 0.0)
        out_ref[part, 0] = total.reshape(size_x, size_y, size_z)


def add_top(operated, cell_add):
    parts, waves, size_x, size_y, size_z = operated.shape
    depth = 128
    block = pl.BlockSpec(
        (parts, 1, size_x, size_y, depth), lambda w: (0, w, 0, 0, size_z // depth - 1)
    )
    return pl.pallas_call(
        top_kernel,
        grid=(waves,),
        in_specs=[block, pl.BlockSpec(cell_add.shape, lambda w: (0, 0))],
        out_specs=block,
        out_shape=jax.ShapeDtypeStruct(operated.shape, jnp.float32),
        input_output_aliases={0: 0},
        cost_estimate=pl.CostEstimate(
            flops=operated.size, bytes_accessed=operated.size * 2, transcendentals=0
        ),
        name="slot_rows",
    )(operated, cell_add)


def stencil(volume, x_lo, x_hi, y_lo, y_hi, edge_lo, edge_hi, coefficients):
    parts, waves, size_x, size_y, size_z = volume.shape
    whole = pl.BlockSpec((parts, 1, size_x, size_y, size_z), lambda w: (0, w, 0, 0, 0))
    face_x = pl.BlockSpec((parts, 1, size_y, size_z), lambda w: (0, w, 0, 0))
    face_y = pl.BlockSpec((parts, 1, size_x, size_z), lambda w: (0, w, 0, 0))
    edge = pl.BlockSpec((parts, 1, 2, size_z), lambda w: (0, w, 0, 0))
    return pl.pallas_call(
        stencil_kernel,
        grid=(waves,),
        in_specs=[
            whole,
            face_x,
            face_x,
            face_y,
            face_y,
            edge,
            edge,
            pl.BlockSpec(coefficients.shape, lambda w: (0, 0, 0, 0)),
        ],
        out_specs=whole,
        out_shape=jax.ShapeDtypeStruct(volume.shape, jnp.float32),
        scratch_shapes=[pltpu.VMEM((parts, size_x + 2, size_y, size_z), jnp.float32)],
        compiler_params=pltpu.CompilerParams(
            vmem_limit_bytes=40 * 1024 * 1024, dimension_semantics=("arbitrary",)
        ),
        cost_estimate=pl.CostEstimate(
            flops=volume.size * 40, bytes_accessed=volume.size * 8, transcendentals=0
        ),
        name="volume_rows",
    )(volume, x_lo, x_hi, y_lo, y_hi, edge_lo, edge_hi, coefficients)


def on_device(
    volume_field,
    coefficients,
    density,
    boundary_matrix,
    upsample,
    trace_cell,
    trace_row,
    slot_counts,
):
    parts, waves, size_x, size_y, size_z = volume_field.shape
    n_wide, n_narrow = lax.axis_size("wide"), lax.axis_size("narrow")
    group_rows = boundary_matrix.shape[2]
    all_rows = n_wide * group_rows
    rows_each = group_rows // n_narrow

    up, down = shifts("wide")
    x_lo = lax.ppermute(volume_field[:, :, -1], "wide", up)
    x_hi = lax.ppermute(volume_field[:, :, 0], "wide", down)

    up_y, down_y = shifts("narrow")
    y_lo = lax.ppermute(volume_field[:, :, :, -1], "narrow", up_y)
    y_hi = lax.ppermute(volume_field[:, :, :, 0], "narrow", down_y)

    partial_rows = bem_partial(density, boundary_matrix, upsample)
    x_lo, x_hi, partial_rows = lax.optimization_barrier((x_lo, x_hi, partial_rows))

    def edges(at):
        return jnp.stack([x_lo[:, :, at], x_hi[:, :, at]], axis=2)

    edge_lo = lax.ppermute(edges(size_y - 1), "narrow", up_y)
    edge_hi = lax.ppermute(edges(0), "narrow", down_y)

    slots = trace_row.shape[2]
    live = jnp.arange(slots, dtype=jnp.int32) < slot_counts.reshape(())
    slot_rows = jnp.where(live, trace_row.reshape(slots), -1)
    slot_cells = trace_cell.reshape(slots)
    row_hot = (slot_rows[None, :] == jnp.arange(all_rows, dtype=jnp.int32)[:, None]).astype(
        jnp.bfloat16
    )
    cell_hot = (
        slot_cells[None, :] == jnp.arange(size_x * size_y, dtype=jnp.int32)[:, None]
    ).astype(jnp.bfloat16)
    counts = lax.dot_general(
        cell_hot, row_hot, (((1,), (1,)), ((), ())), preferred_element_type=jnp.float32
    )
    top = volume_field[:, :, :, :, -1].reshape(parts * waves, size_x * size_y)
    trace_part = jnp.dot(top, counts, precision=lax.Precision.HIGHEST)
    trace_part = trace_part.reshape(parts * waves, n_wide * n_narrow, rows_each)
    trace_part = trace_part.transpose(1, 0, 2).reshape(n_wide * n_narrow, -1)
    devices = n_wide * n_narrow
    flat = partial_rows.size
    outgoing = jnp.concatenate(
        [jnp.broadcast_to(partial_rows.reshape(1, flat), (devices, flat)), trace_part], axis=1
    )
    arrived = lax.all_to_all(
        outgoing.reshape(devices, 1, -1), BOTH, split_axis=0, concat_axis=0, tiled=True
    ).reshape(devices, -1)
    trace_sum = jnp.sum(arrived[:, flat:], axis=0).reshape(parts * waves, rows_each)
    gathered = arrived[:, :flat]
    summed = jnp.sum(gathered.reshape(n_wide, n_narrow, waves, 2, group_rows), axis=1)
    bem_rows = summed.transpose(2, 1, 0, 3).reshape(parts * waves, all_rows)
    start = (lax.axis_index("wide") * n_narrow + lax.axis_index("narrow")) * rows_each
    own_rows = lax.dynamic_slice_in_dim(bem_rows, start, rows_each, 1)
    boundary_out = (own_rows - 0.25 * trace_sum).reshape(parts, waves, rows_each)
    cell_add = lax.dot_general(
        counts, bem_rows, (((1,), (1,)), ((), ())), precision=lax.Precision.HIGHEST
    )
    operated = stencil(volume_field, x_lo, x_hi, y_lo, y_hi, edge_lo, edge_hi, coefficients)
    volume_out = add_top(operated, cell_add)
    return (volume_out, boundary_out)


def solution(mesh):
    return jax.shard_map(
        on_device,
        mesh=mesh,
        in_specs=(
            P(None, None, "wide", "narrow", None),
            P(None, "wide", "narrow", None),
            P(None, None, "narrow"),
            P(None, None, "wide", "narrow"),
            P("narrow"),
            P("wide", "narrow", None),
            P("wide", "narrow", None),
            P("wide", "narrow"),
        ),
        out_specs=(P(None, None, "wide", "narrow", None), P(None, None, ("wide", "narrow"))),
        check_vma=False,
    )
```

```python
import functools

import jax
import jax.numpy as jnp
from jax import lax
from jax.experimental import pallas as pl
from jax.experimental.pallas import tpu as pltpu
from jax.sharding import PartitionSpec as P

UMAX = 4
BOTH = ("wide", "narrow")


def shifts(axis):
    peers = lax.axis_size(axis)
    up = [(i, i + 1) for i in range(peers - 1)]
    return up, [(j, i) for i, j in up]


def bem_kernel(keep_ref, next_ref, density_ref, matrix_ref, out_ref, *, groups, width):
    step = pl.program_id(0)
    waves = density_ref.shape[1]
    rows = matrix_ref.shape[2]
    lane = lax.broadcasted_iota(jnp.int32, (2 * waves, width), 1)
    total = jnp.zeros((2 * waves, 2 * rows), jnp.float32)
    for g in range(groups):
        columns = pl.ds(g * width, width)
        own = density_ref[:, :, columns].reshape(2 * waves, width)
        after = jnp.where(lane == width - 1, own, pltpu.roll(own, width - 1, axis=1))
        for level in range(UMAX):
            at = step * groups + g
            fine = keep_ref[level, at] * own + next_ref[level, at] * after
            matrix = matrix_ref[:, level, :, columns].reshape(2 * rows, width)
            total = total + lax.dot_general(
                fine.astype(jnp.bfloat16),
                matrix,
                (((1,), (1,)), ((), ())),
                preferred_element_type=jnp.float32,
            )
    real = total[:waves, :rows] - total[waves:, rows:]
    imag = total[waves:, :rows] + total[:waves, rows:]
    packed = jnp.concatenate([real, imag], axis=1)

    @pl.when(step == 0)
    def _():
        out_ref[...] = packed

    @pl.when(step > 0)
    def _():
        out_ref[...] += packed


def bem_partial(density, boundary_matrix, upsample):
    parts, waves, columns = density.shape
    rows = boundary_matrix.shape[2]
    blocks = upsample.shape[0]
    width = columns // blocks
    groups = 4 if blocks % 4 == 0 else 1
    factor = upsample.astype(jnp.float32)[None, :]
    level = jnp.arange(UMAX, dtype=jnp.int32)[:, None]
    blend = level.astype(jnp.float32) / factor
    used = level < upsample[None, :]
    keep = jnp.where(used, (1.0 - blend) / factor, 0.0)
    following = jnp.where(used, blend / factor, 0.0)


    return pl.pallas_call(
        functools.partial(bem_kernel, groups=groups, width=width),
        grid=(blocks // groups,),
        in_specs=[
            pl.BlockSpec(memory_space=pltpu.SMEM),
            pl.BlockSpec(memory_space=pltpu.SMEM),
            pl.BlockSpec((parts, waves, groups * width), lambda i: (0, 0, i)),
            pl.BlockSpec((2, UMAX, rows, groups * width), lambda i: (0, 0, 0, i)),
        ],
        out_specs=pl.BlockSpec((waves, 2 * rows), lambda i: (0, 0)),
        out_shape=jax.ShapeDtypeStruct((waves, 2 * rows), jnp.float32),
        compiler_params=pltpu.CompilerParams(
            vmem_limit_bytes=56 * 1024 * 1024, dimension_semantics=("arbitrary",)
        ),
        cost_estimate=pl.CostEstimate(
            flops=2 * UMAX * 4 * waves * rows * columns,
            bytes_accessed=boundary_matrix.size * 2 + density.size * 4,
            transcendentals=0,
        ),
        name="boundary_product",
    )(keep, following, density, boundary_matrix)


def stencil_kernel(
    volume_ref, x_lo, x_hi, y_lo, y_hi, edge_lo, edge_hi, scale_ref, out_ref, across_ref
):
    size_x, size_y, size_z = volume_ref.shape[2:]
    shape = (size_y, size_z)
    row = lax.broadcasted_iota(jnp.int32, shape, 0)
    lane = lax.broadcasted_iota(jnp.int32, shape, 1)

    def sum_y(plane, before, after):
        up = jnp.where(row == 0, before, pltpu.roll(plane, 1, axis=0))
        down = jnp.where(row == size_y - 1, after, pltpu.roll(plane, size_y - 1, axis=0))
        return up + down

    for part in range(2):
        for side, face, at in ((0, x_lo, 0), (1, x_hi, size_x + 1)):
            across_ref[part, at] = sum_y(
                face[part, 0], edge_lo[part, 0, side : side + 1], edge_hi[part, 0, side : side + 1]
            )

    def first(x, carry):
        for part in range(2):
            across_ref[part, x + 1] = sum_y(
                volume_ref[part, 0, x],
                y_lo[part, 0, pl.ds(x, 1), :],
                y_hi[part, 0, pl.ds(x, 1), :],
            )
        return carry

    lax.fori_loop(0, size_x, first, 0)

    def emit(x, before, after):
        scale0 = scale_ref[0, x].astype(jnp.float32)
        scale1 = scale_ref[1, x].astype(jnp.float32)
        scale2 = scale_ref[2, x].astype(jnp.float32)
        own = [volume_ref[part, 0, x] for part in range(2)]
        for part in range(2):
            outer = across_ref[part, x] + across_ref[part, x + 2]
            inner = outer + 2.0 * (before[part] + after[part] + across_ref[part, x + 1])
            left = jnp.where(lane == 0, 0.0, pltpu.roll(inner, 1, axis=1))
            right = jnp.where(lane == size_z - 1, 0.0, pltpu.roll(inner, size_z - 1, axis=1))
            total = left + right + 2.0 * outer
            stiffness = (8.0 / 3.0) * own[part] - total * (1.0 / 12.0)
            turned = own[1] if part == 0 else -own[0]
            out_ref[part, 0, x] = scale0 * stiffness - scale1 * own[part] + scale2 * turned

    both = range(2)
    emit(0, [x_lo[p, 0] for p in both], [volume_ref[p, 0, 1] for p in both])

    def second(x, carry):
        emit(
            x,
            [volume_ref[p, 0, x - 1] for p in both],
            [volume_ref[p, 0, x + 1] for p in both],
        )
        return carry

    lax.fori_loop(1, size_x - 1, second, 0)
    emit(
        size_x - 1,
        [volume_ref[p, 0, size_x - 2] for p in both],
        [x_hi[p, 0] for p in both],
    )


def top_kernel(operated_ref, add_ref, out_ref):
    wave = pl.program_id(0)
    waves = pl.num_programs(0)
    size_x, size_y, size_z = operated_ref.shape[2:]
    cells = size_x * size_y
    channels = add_ref.shape[1]
    channel = lax.broadcasted_iota(jnp.int32, (channels, size_z), 0)
    lane = lax.broadcasted_iota(jnp.int32, (channels, size_z), 1)
    for part in range(2):
        pick = (channel == part * waves + wave) & (lane == size_z - 1)
        added = jnp.dot(
            add_ref[...],
            pick.astype(jnp.float32),
            precision=lax.Precision.HIGHEST,
            preferred_element_type=jnp.float32,
        )
        out_ref[part, 0] = operated_ref[part, 0] + added.reshape(size_x, size_y, size_z)


def add_top(operated, cell_add):
    parts, waves, size_x, size_y, size_z = operated.shape
    depth = 128
    block = pl.BlockSpec(
        (parts, 1, size_x, size_y, depth), lambda w: (0, w, 0, 0, size_z // depth - 1)
    )
    return pl.pallas_call(
        top_kernel,
        grid=(waves,),
        in_specs=[block, pl.BlockSpec(cell_add.shape, lambda w: (0, 0))],
        out_specs=block,
        out_shape=jax.ShapeDtypeStruct(operated.shape, jnp.float32),
        input_output_aliases={0: 0},
        cost_estimate=pl.CostEstimate(
            flops=operated.size, bytes_accessed=operated.size * 2, transcendentals=0
        ),
        name="slot_rows",
    )(operated, cell_add)


def stencil(volume, x_lo, x_hi, y_lo, y_hi, edge_lo, edge_hi, coefficients):
    parts, waves, size_x, size_y, size_z = volume.shape
    whole = pl.BlockSpec((parts, 1, size_x, size_y, size_z), lambda w: (0, w, 0, 0, 0))
    face_x = pl.BlockSpec((parts, 1, size_y, size_z), lambda w: (0, w, 0, 0))
    face_y = pl.BlockSpec((parts, 1, size_x, size_z), lambda w: (0, w, 0, 0))
    edge = pl.BlockSpec((parts, 1, 2, size_z), lambda w: (0, w, 0, 0))
    return pl.pallas_call(
        stencil_kernel,
        grid=(waves,),
        in_specs=[
            whole,
            face_x,
            face_x,
            face_y,
            face_y,
            edge,
            edge,
            pl.BlockSpec(coefficients.shape, lambda w: (0, 0, 0, 0)),
        ],
        out_specs=whole,
        out_shape=jax.ShapeDtypeStruct(volume.shape, jnp.float32),
        scratch_shapes=[pltpu.VMEM((parts, size_x + 2, size_y, size_z), jnp.float32)],
        compiler_params=pltpu.CompilerParams(
            vmem_limit_bytes=56 * 1024 * 1024, dimension_semantics=("arbitrary",)
        ),
        cost_estimate=pl.CostEstimate(
            flops=volume.size * 40, bytes_accessed=volume.size * 8, transcendentals=0
        ),
        name="volume_rows",
    )(volume, x_lo, x_hi, y_lo, y_hi, edge_lo, edge_hi, coefficients)


def on_device(
    volume_field,
    coefficients,
    density,
    boundary_matrix,
    upsample,
    trace_cell,
    trace_row,
    slot_counts,
):
    parts, waves, size_x, size_y, size_z = volume_field.shape
    n_wide, n_narrow = lax.axis_size("wide"), lax.axis_size("narrow")
    group_rows = boundary_matrix.shape[2]
    all_rows = n_wide * group_rows
    rows_each = group_rows // n_narrow

    up, down = shifts("wide")
    x_last, x_first, later = lax.optimization_barrier(
        (volume_field[:, :, -1], volume_field[:, :, 0], volume_field)
    )
    x_lo = lax.ppermute(x_last, "wide", up)
    x_hi = lax.ppermute(x_first, "wide", down)
    up_y, down_y = shifts("narrow")
    y_lo = lax.ppermute(later[:, :, :, -1], "narrow", up_y)
    y_hi = lax.ppermute(later[:, :, :, 0], "narrow", down_y)

    partial_rows = bem_partial(density, boundary_matrix, upsample)
    x_lo, x_hi, partial_rows = lax.optimization_barrier((x_lo, x_hi, partial_rows))

    def edges(at):
        return jnp.stack([x_lo[:, :, at], x_hi[:, :, at]], axis=2)

    edge_lo = lax.ppermute(edges(size_y - 1), "narrow", up_y)
    edge_hi = lax.ppermute(edges(0), "narrow", down_y)

    slots = trace_row.shape[2]
    live = jnp.arange(slots, dtype=jnp.int32) < slot_counts.reshape(())
    slot_rows = jnp.where(live, trace_row.reshape(slots), -1)
    slot_cells = trace_cell.reshape(slots)
    row_hot = (slot_rows[None, :] == jnp.arange(all_rows, dtype=jnp.int32)[:, None]).astype(
        jnp.bfloat16
    )
    cell_hot = (
        slot_cells[None, :] == jnp.arange(size_x * size_y, dtype=jnp.int32)[:, None]
    ).astype(jnp.bfloat16)
    counts = lax.dot_general(
        cell_hot, row_hot, (((1,), (1,)), ((), ())), preferred_element_type=jnp.float32
    )
    top = volume_field[:, :, :, :, -1].reshape(parts * waves, size_x * size_y)
    trace_part = jnp.dot(top, counts, precision=lax.Precision.HIGHEST)
    trace_part = trace_part.reshape(parts * waves, n_wide * n_narrow, rows_each)
    trace_part = trace_part.transpose(1, 0, 2).reshape(n_wide * n_narrow, -1)
    devices = n_wide * n_narrow
    flat = partial_rows.size
    outgoing = jnp.concatenate(
        [jnp.broadcast_to(partial_rows.reshape(1, flat), (devices, flat)), trace_part], axis=1
    )
    arrived = lax.all_to_all(
        outgoing.reshape(devices, 1, -1), BOTH, split_axis=0, concat_axis=0, tiled=True
    ).reshape(devices, -1)
    trace_sum = jnp.sum(arrived[:, flat:], axis=0).reshape(parts * waves, rows_each)
    gathered = arrived[:, :flat]
    summed = jnp.sum(gathered.reshape(n_wide, n_narrow, waves, 2, group_rows), axis=1)
    bem_rows = summed.transpose(2, 1, 0, 3).reshape(parts * waves, all_rows)
    start = (lax.axis_index("wide") * n_narrow + lax.axis_index("narrow")) * rows_each
    own_rows = lax.dynamic_slice_in_dim(bem_rows, start, rows_each, 1)
    boundary_out = (own_rows - 0.25 * trace_sum).reshape(parts, waves, rows_each)
    cell_add = lax.dot_general(
        counts, bem_rows, (((1,), (1,)), ((), ())), precision=lax.Precision.HIGHEST
    )
    operated = stencil(volume_field, x_lo, x_hi, y_lo, y_hi, edge_lo, edge_hi, coefficients)
    volume_out = add_top(operated, cell_add)
    return (volume_out, boundary_out)


def solution(mesh):
    return jax.shard_map(
        on_device,
        mesh=mesh,
        in_specs=(
            P(None, None, "wide", "narrow", None),
            P(None, "wide", "narrow", None),
            P(None, None, "narrow"),
            P(None, None, "wide", "narrow"),
            P("narrow"),
            P("wide", "narrow", None),
            P("wide", "narrow", None),
            P("wide", "narrow"),
        ),
        out_specs=(P(None, None, "wide", "narrow", None), P(None, None, ("wide", "narrow"))),
        check_vma=False,
    )
```
